1024 devices in a mesh: dp: 128 (over z, x_hi, core), tensor: 8 (over y, x_lo).
Axes of the slice: x: 4 (x_hi: 2, x_lo: 2; x = x_hi * 2 + x_lo), y: 4, z: 32, core: 2. Of those that a mesh axis runs over, the one named last changes fastest.
Arguments:
- tokens: bfloat16 [256, 8192], P(None, 'tensor'), may hold values from -6 to 6
- cotangent: bfloat16 [256, 8192], P(None, 'tensor'), may hold values from -6 to 6
- text_count: int32 [128], replicated, may hold values from 0 to 2, as said below
- w_gate: bfloat16 [2, 8192, 11008], P(None, 'tensor', 'dp'), may hold values from -0.0625 to 0.0625
- w_up: bfloat16 [2, 8192, 11008], P(None, 'tensor', 'dp'), may hold values from -0.0625 to 0.0625
- w_down: bfloat16 [2, 11008, 8192], P(None, 'dp', 'tensor'), may hold values from -0.0546875 to 0.0546875
Outputs:
- mixed: bfloat16 [256, 8192], P('dp', 'tensor')
- grad_tokens: bfloat16 [256, 8192], P('dp', 'tensor')
- grad_gate: float32 [2, 8192, 11008], P(None, 'tensor', 'dp')
- grad_up: float32 [2, 8192, 11008], P(None, 'tensor', 'dp')
- grad_down: float32 [2, 11008, 8192], P(None, 'dp', 'tensor')
The draws below stay inside these ranges and needn't reach their ends.
Inputs may be any that keep to these rules, and one draw needn't show every extreme that they name: In group s the first text_count[s] tokens are text and the others image; some group is all text and some all image.
All inputs are finite; a program needn't handle non-finite values.
Results may differ from the reference program's by a relative error of at most 0.005.
Values may be sent and summed in bfloat16 or wider, within the bound.
No kernel may reach another device: no remote copies, remote signals or barrier semaphores. Data moves between devices by JAX's collectives and lax.ppermute only.
A program may use at most 32 MiB of HBM per device.

```python
import jax
import jax.numpy as jnp
from jax import lax

D = 8192
FF = 11008
TOK_DEV = 2
TOKENS = 256
N_DP = 128


def draw_text_count(key, part):
    key = jax.random.fold_in(key, 7)
    first_key, second_key = jax.random.split(key)
    counts = jax.random.randint(first_key, (N_DP,), 0, TOK_DEV + 1, dtype=jnp.int32)
    places = jax.random.permutation(second_key, N_DP)
    counts = counts.at[places[0]].set(TOK_DEV)
    return counts.at[places[1]].set(0)


def level_of(key, shape, shards, smallest, top_value):
    def one(axis_at, shards_of):
        draws = jax.random.uniform(jax.random.fold_in(jax.random.fold_in(key, 6), axis_at), (shards_of,), jnp.float32, smallest / len(shards), top_value / len(shards))
        return jnp.repeat(jnp.exp(draws), shape[axis_at] // shards_of).reshape((-1,) + (1,) * (len(shape) - axis_at - 1))

    loudness = one(*shards[0])
    for cut in shards[1:]:
        loudness = loudness * one(*cut)
    return loudness


def gaussian(key, dims, spread, bound, cuts=(), kind=jnp.bfloat16):
    entries = spread * jax.random.normal(key, dims, jnp.float32)
    if cuts:
        entries = entries * level_of(key, dims, cuts, -0.22, 0.18)
    return jnp.clip(entries, -bound, bound).astype(kind)


def setup_inputs(seed: int = 0) -> dict:
    arg_keys = jax.random.split(jax.random.key(seed), 7)
    tokens = gaussian(arg_keys[0], (TOKENS, D), 1.0, 6.0, ((1, 8),))
    cotangent = gaussian(arg_keys[1], (TOKENS, D), 1.0, 6.0, ((1, 8),))
    text_count = draw_text_count(jax.random.fold_in(arg_keys[6], 71), 0)
    w_gate = gaussian(arg_keys[3], (2, D, FF), D ** -0.5, 0.0625, ((1, 8), (2, 128)))
    w_up = gaussian(arg_keys[4], (2, D, FF), D ** -0.5, 0.0625, ((1, 8), (2, 128)))
    w_down = gaussian(arg_keys[5], (2, FF, D), FF ** -0.5, 0.0546875, ((1, 128), (2, 8)))
    return dict(tokens=tokens, cotangent=cotangent, text_count=text_count, w_gate=w_gate, w_up=w_up, w_down=w_down)


def transposed_dot(left, right):
    return lax.dot_general(left, right, (((0,), (0,)), ((), ())), preferred_element_type=jnp.float32)


def against(left, right):
    return lax.dot_general(left, right, (((1,), (1,)), ((), ())), preferred_element_type=jnp.float32)


def reference(tokens, cotangent, text_count, w_gate, w_up, w_down):
    rows = jnp.arange(TOKENS, dtype=jnp.int32)
    is_text = (rows % TOK_DEV) < text_count[rows // TOK_DEV]
    column = is_text[:, None]
    zero = jnp.zeros((), tokens.dtype)

    def pick(first, second):
        return jnp.where(column, first, second)

    gate = pick(jnp.dot(tokens, w_gate[0], preferred_element_type=jnp.float32),
                jnp.dot(tokens, w_gate[1], preferred_element_type=jnp.float32))
    up = pick(jnp.dot(tokens, w_up[0], preferred_element_type=jnp.float32),
              jnp.dot(tokens, w_up[1], preferred_element_type=jnp.float32))
    sig = jax.nn.sigmoid(gate)
    act = gate * sig
    hidden = (act * up).astype(jnp.bfloat16)
    mixed = pick(jnp.dot(hidden, w_down[0], preferred_element_type=jnp.float32),
                 jnp.dot(hidden, w_down[1], preferred_element_type=jnp.float32)).astype(jnp.bfloat16)
    grad_hidden = pick(against(cotangent, w_down[0]), against(cotangent, w_down[1]))
    grad_gate_rows = (grad_hidden * up * sig * (1.0 + gate * (1.0 - sig))).astype(jnp.bfloat16)
    grad_up_rows = (grad_hidden * act).astype(jnp.bfloat16)
    grad_tokens = pick(against(grad_gate_rows, w_gate[0]) + against(grad_up_rows, w_up[0]),
                       against(grad_gate_rows, w_gate[1]) + against(grad_up_rows, w_up[1])).astype(jnp.bfloat16)
    hidden_zero = jnp.zeros((), hidden.dtype)
    grad_down = jnp.stack((transposed_dot(jnp.where(column, hidden, hidden_zero), cotangent),
                           transposed_dot(jnp.where(column, hidden_zero, hidden), cotangent)))
    text_tokens = jnp.where(column, tokens, zero)
    image_tokens = jnp.where(column, zero, tokens)
    grad_gate = jnp.stack((transposed_dot(text_tokens, grad_gate_rows), transposed_dot(image_tokens, grad_gate_rows)))
    grad_up = jnp.stack((transposed_dot(text_tokens, grad_up_rows), transposed_dot(image_tokens, grad_up_rows)))
    return mixed, grad_tokens, grad_gate, grad_up, grad_down
```

```python
import jax
import jax.numpy as jnp
from jax import lax
from jax.sharding import Mesh, PartitionSpec as P

BF16 = jnp.bfloat16
F32 = jnp.float32
LANES = 128


def dp_parts(n):
    z = n // 4
    z_lo = 4 if z % 4 == 0 else 2
    return z // z_lo, z_lo, 2, 2


def transposed_dot(left, right):
    return lax.dot_general(left, right, (((0,), (0,)), ((), ())), preferred_element_type=F32)


def contract_last(left, right, right_dim):
    return lax.dot_general(left, right, (((1,), (right_dim,)), ((), ())), preferred_element_type=F32)


def text_rows(text_count, total):
    groups = text_count.shape[0]
    tok_group = total // groups
    rows = jnp.arange(total, dtype=jnp.int32)
    onehot = (rows // tok_group)[:, None] == jnp.arange(groups, dtype=jnp.int32)[None, :]
    limit = jnp.sum(jnp.where(onehot, text_count[None, :], 0), axis=1)
    return rows % tok_group < limit


def masked_rows(left, weights, is_text, right_dim):
    first = contract_last(left, weights[0], right_dim)
    second = contract_last(left, weights[1], right_dim)
    return jnp.where(is_text[:, None], first, second)


def masked_weight_grads(left, right, is_text):
    zero = jnp.zeros((), left.dtype)
    column = is_text[:, None]
    return jnp.stack(
        (
            transposed_dot(jnp.where(column, left, zero), right),
            transposed_dot(jnp.where(column, zero, left), right),
        )
    )


def padded(x):
    return jnp.pad(x, ((0, 0), (0, LANES - x.shape[1])))


def program(sizes):
    n_zh, n_zl, n_xh, n_core, n_tensor = sizes
    near = n_zl * n_xh

    def by_core(x, total):
        t = total // (n_zh * near * n_core)
        y = x.reshape((n_zh, near, n_core, t) + x.shape[1:])
        return jnp.transpose(y, (2, 1, 0, 3) + tuple(range(4, y.ndim))).reshape(x.shape)

    def on_device(tokens, cotangent, text_count, w_gate, w_up, w_down):
        total, features = tokens.shape
        width = w_gate.shape[2]
        is_text = text_rows(text_count, total)
        partial = jnp.concatenate(
            (
                padded(masked_rows(tokens, w_gate, is_text, 0)),
                padded(masked_rows(tokens, w_up, is_text, 0)),
                padded(masked_rows(cotangent, w_down, is_text, 1)),
            ),
            axis=1,
        ).reshape(n_tensor, total // n_tensor, 3 * LANES)
        shares = lax.all_to_all(partial, "tensor", 0, 0)
        share = jnp.sum(shares, axis=0)
        gate = share[:, :LANES]
        up = share[:, LANES : 2 * LANES]
        grad_share = share[:, 2 * LANES :]
        sig = jax.nn.sigmoid(gate)
        act = gate * sig
        rows = jnp.concatenate(
            (
                (act * up).astype(BF16),
                (grad_share * up * sig * (1.0 + gate * (1.0 - sig))).astype(BF16),
                (grad_share * act).astype(BF16),
            ),
            axis=1,
        )
        copies = jnp.broadcast_to(rows[None], (n_tensor,) + rows.shape)
        every = lax.all_to_all(copies, "tensor", 0, 0).reshape(total, 3 * LANES)
        hidden = every[:, :width]
        grad_gate_rows = every[:, LANES : LANES + width]
        grad_up_rows = every[:, 2 * LANES : 2 * LANES + width]

        sorted_rows = by_core(every, total)
        sorted_text = by_core(is_text, total)
        mixed = masked_rows(sorted_rows[:, :width], w_down, sorted_text, 0)
        grad_tokens = masked_rows(
            sorted_rows[:, LANES : LANES + width], w_gate, sorted_text, 1
        ) + masked_rows(sorted_rows[:, 2 * LANES : 2 * LANES + width], w_up, sorted_text, 1)
        both = jnp.concatenate((mixed, grad_tokens), axis=1)
        core = lax.axis_index("core")
        half = total // n_core
        keep = lax.dynamic_slice_in_dim(both, core * half, half, 0)
        send = lax.dynamic_slice_in_dim(both, (1 - core) * half, half, 0).astype(BF16)
        got = lax.ppermute(send, "core", [(0, 1), (1, 0)])
        chip = (keep + got.astype(F32)).astype(BF16)
        chip = chip.reshape(near, half // near, 2 * features)
        parts = lax.all_to_all(chip, ("zl", "xh"), 0, 0)
        mine = jnp.sum(parts.astype(F32), axis=0).astype(BF16)
        mine = mine.reshape(n_zh, half // near // n_zh, 2 * features)
        parts = lax.all_to_all(mine, "zh", 0, 0)
        out = jnp.sum(parts.astype(F32), axis=0).astype(BF16)

        grad_down = masked_weight_grads(hidden, cotangent, is_text)
        grad_gate = masked_weight_grads(tokens, grad_gate_rows, is_text)
        grad_up = masked_weight_grads(tokens, grad_up_rows, is_text)
        return out[:, :features], out[:, features:], grad_gate, grad_up, grad_down

    return on_device


def solution(mesh):
    n_dp, n_tensor = mesh.shape["dp"], mesh.shape["tensor"]
    sizes = dp_parts(n_dp) + (n_tensor,)
    split = Mesh(mesh.devices.reshape(sizes), ("zh", "zl", "xh", "core", "tensor"))
    dp = ("zh", "zl", "xh", "core")
    return jax.shard_map(
        program(sizes),
        mesh=split,
        in_specs=(
            P(None, "tensor"),
            P(None, "tensor"),
            P(),
            P(None, "tensor", dp),
            P(None, "tensor", dp),
            P(None, dp, "tensor"),
        ),
        out_specs=(
            P(dp, "tensor"),
            P(dp, "tensor"),
            P(None, "tensor", dp),
            P(None, "tensor", dp),
            P(None, dp, "tensor"),
        ),
        check_vma=False,
    )
```

```python
import functools

import jax
import jax.numpy as jnp
from jax import lax
from jax.experimental import pallas as pl
from jax.experimental.pallas import tpu as pltpu
from jax.sharding import PartitionSpec as P

BF16 = jnp.bfloat16
F32 = jnp.float32
I32 = jnp.int32
LANES = 128
VMEM = pl.BlockSpec(memory_space=pltpu.VMEM)
SMEM = pl.BlockSpec(memory_space=pltpu.SMEM)


def dp_parts(n):
    z = n // 4
    z_lo = 4 if z >= 16 else 2
    return z // z_lo, z_lo


def near_members(n_zh, n_zl):
    return [((a + 1) % n_zl, x) for a in range(n_zl) for x in range(2)]


def far_members(n_zh, n_zl):
    return [(a + n_zh // 2) % n_zh for a in range(n_zh)]


def groups_of(n_zh, n_zl):
    near = [
        [((h * n_zl + low) * 2 + x) * 2 + c for low, x in near_members(n_zh, n_zl)]
        for h in range(n_zh)
        for c in range(2)
    ]
    far = [
        [((h * n_zl + low) * 2 + x) * 2 + c for h in far_members(n_zh, n_zl)]
        for low in range(n_zl)
        for x in range(2)
        for c in range(2)
    ]
    return near, far


def iota(shape, dim):
    return lax.broadcasted_iota(I32, shape, dim)


def dot(left, right, dims=((1,), (0,))):
    return lax.dot_general(left, right, (dims, ((), ())), preferred_element_type=F32)


def partial_kernel(tok_ref, cot_ref, count_ref, gate_ref, up_ref, down_ref, out_ref, both, one):
    total, features = tok_ref.shape
    width = gate_ref.shape[0]
    n_groups = count_ref.shape[1]
    spread = (iota((n_groups, total), 1) // 2 == iota((n_groups, total), 0)).astype(BF16)
    counts = jnp.broadcast_to(count_ref[...].astype(F32), (8, n_groups)).astype(BF16)
    limit = dot(counts, spread)[0:1, :]
    is_text = (iota((1, total), 1) % 2).astype(F32) < limit
    one[...] = jnp.zeros_like(one)
    for j, (left, weight) in enumerate(
        ((tok_ref, gate_ref), (tok_ref, up_ref), (cot_ref, down_ref))
    ):
        rows = weight[...].reshape(2 * width, features)
        products = dot(rows, left[...], ((1,), (1,)))
        n, _, lanes = both.shape
        for c in range(n):
            here = slice(c * lanes, (c + 1) * lanes)
            both[c] = products[:, here]
            text = both[c, pl.ds(0, width, 2), :]
            image = both[c, pl.ds(1, width, 2), :]
            one[0:width, here] = jnp.where(is_text[:, here], text, image)
        out_ref[:, j * LANES : (j + 1) * LANES] = one[...].T


def interleaved(rows, is_text, width):
    n = rows.shape[0]
    expand = (iota((LANES, 2 * width), 1) // 2 == iota((LANES, 2 * width), 0)).astype(BF16)
    wide = dot(rows, expand)
    is_even = iota((n, 2 * width), 1) % 2 == 0
    return jnp.where(is_even == is_text, wide, 0.0).astype(BF16)


def text_column(row, count_ref):
    n, n_groups = row.shape[0], count_ref.shape[1]
    hit = iota((n, n_groups), 1) == row // 2
    limit = jnp.sum(
        jnp.where(hit, count_ref[...].astype(F32), 0.0), axis=1, keepdims=True
    )
    return (row % 2).astype(F32) < limit


def sums_kernel(n_zh, n_zl, core_ref, rows_ref, count_ref, gate_ref, up_ref, down_ref, keep_ref, send_ref):
    total = rows_ref.shape[0]
    width, _, features = gate_ref.shape
    half = total // 2
    core = core_ref[0]
    q = iota((total, 1), 0)
    side = jnp.where(q < half, core, 1 - core)
    i = q % half
    per = 2 * n_zh
    d = i // per
    far = i % per // 2
    low = (d // 2 + 1) % n_zl
    high = (far + n_zh // 2) % n_zh
    row = ((high * n_zl + low) * 2 + d % 2) * 4 + side * 2 + i % 2
    is_text = text_column(row, count_ref)
    pick = (iota((total, total), 1) == row).astype(BF16)
    rows = dot(pick, rows_ref[...]).astype(BF16)

    def wide(j):
        return interleaved(rows[:, j * LANES : (j + 1) * LANES], is_text, width)

    mixed = dot(wide(0), down_ref[...].reshape(2 * width, features))
    keep_ref[:, :features] = mixed[:half]
    send_ref[:, :features] = mixed[half:].astype(BF16)
    grad = dot(wide(1), gate_ref[...].reshape(2 * width, features)) + dot(
        wide(2), up_ref[...].reshape(2 * width, features)
    )
    keep_ref[:, features:] = grad[:half]
    send_ref[:, features:] = grad[half:].astype(BF16)


def weight_grads_kernel(rows_ref, count_ref, tok_ref, cot_ref, gate_ref, up_ref, down_ref):
    total, features = tok_ref.shape
    width = gate_ref.shape[0]
    is_text = text_column(iota((total, 1), 0), count_ref)
    for j, (left, out) in enumerate(
        ((cot_ref, down_ref), (tok_ref, gate_ref), (tok_ref, up_ref))
    ):
        wide = interleaved(rows_ref[:, j * LANES : (j + 1) * LANES], is_text, width)
        out[...] = dot(wide, left[...], ((0,), (0,))).reshape(width, 2, features)


def program(n_zh, n_zl, n_tensor):
    near, far = groups_of(n_zh, n_zl)
    n_near = 2 * n_zl

    def on_device(tokens, cotangent, text_count, w_gate, w_up, w_down):
        total, features = tokens.shape
        width = w_gate.shape[2]
        half = total // 2
        lanes = min(total, LANES)
        counts = text_count.reshape(1, -1)
        gate_w = jnp.transpose(w_gate, (2, 0, 1))
        up_w = jnp.transpose(w_up, (2, 0, 1))
        down_w = jnp.transpose(w_down, (1, 0, 2))
        params = pltpu.CompilerParams(vmem_limit_bytes=24 * 1024 * 1024)
        partial = pl.pallas_call(
            partial_kernel,
            out_shape=jax.ShapeDtypeStruct((total, 3 * LANES), F32),
            in_specs=[VMEM] * 6,
            out_specs=VMEM,
            scratch_shapes=[
                pltpu.VMEM((total // lanes, 2 * width, lanes), F32),
                pltpu.VMEM((LANES, total), F32),
            ],
            compiler_params=params,
            name="partial_sums",
        )(tokens, cotangent, counts, gate_w, up_w, down_w)
        partial = partial.reshape(n_tensor, total // n_tensor, 3 * LANES)
        share = jnp.sum(lax.all_to_all(partial, "tensor", 0, 0), axis=0)
        gate = share[:, :LANES]
        up = share[:, LANES : 2 * LANES]
        grad_hidden = share[:, 2 * LANES :]
        sig = jax.nn.sigmoid(gate)
        act = gate * sig
        rows = jnp.concatenate(
            (
                (act * up).astype(BF16),
                (grad_hidden * up * sig * (1.0 + gate * (1.0 - sig))).astype(BF16),
                (grad_hidden * act).astype(BF16),
            ),
            axis=1,
        )
        copies = jnp.broadcast_to(rows[None], (n_tensor,) + rows.shape)
        rows = lax.all_to_all(copies, "tensor", 0, 0).reshape(total, 3 * LANES)

        core = (lax.axis_index("dp") % 2).astype(I32).reshape(1)
        keep, send = pl.pallas_call(
            functools.partial(sums_kernel, n_zh, n_zl),
            out_shape=(
                jax.ShapeDtypeStruct((half, 2 * features), F32),
                jax.ShapeDtypeStruct((half, 2 * features), BF16),
            ),
            in_specs=[SMEM] + [VMEM] * 5,
            out_specs=(VMEM, VMEM),
            compiler_params=params,
            name="token_sums",
        )(core, rows, counts, gate_w, up_w, down_w)
        n_dp = 4 * n_zh * n_zl
        got = lax.ppermute(send, "dp", [(i, i ^ 1) for i in range(n_dp)])
        chip = (keep + got.astype(F32)).astype(BF16)
        chip = chip.reshape(n_near, half // n_near, 2 * features)
        parts = lax.all_to_all(chip, "dp", 0, 0, axis_index_groups=near)
        grads = pl.pallas_call(
            weight_grads_kernel,
            out_shape=(jax.ShapeDtypeStruct((width, 2, features), F32),) * 3,
            in_specs=[VMEM] * 4,
            out_specs=(VMEM,) * 3,
            compiler_params=params,
            cost_estimate=pl.CostEstimate(
                flops=12 * total * width * features, bytes_accessed=4 << 20, transcendentals=0
            ),
            name="weight_grads",
        )(rows, counts, tokens, cotangent)
        mine = jnp.sum(parts.astype(F32), axis=0).astype(BF16)
        mine = mine.reshape(n_zh, 2, 2 * features)
        mine, gate_g, up_g, down_g = lax.optimization_barrier((mine,) + tuple(grads))
        parts = lax.all_to_all(mine, "dp", 0, 0, axis_index_groups=far)
        out = jnp.sum(parts.astype(F32), axis=0).astype(BF16)
        return (
            out[:, :features],
            out[:, features:],
            jnp.transpose(gate_g, (1, 2, 0)),
            jnp.transpose(up_g, (1, 2, 0)),
            jnp.transpose(down_g, (1, 0, 2)),
        )

    return on_device


def solution(mesh):
    n_zh, n_zl = dp_parts(mesh.shape["dp"])
    return jax.shard_map(
        program(n_zh, n_zl, mesh.shape["tensor"]),
        mesh=mesh,
        in_specs=(
            P(None, "tensor"),
            P(None, "tensor"),
            P(),
            P(None, "tensor", "dp"),
            P(None, "tensor", "dp"),
            P(None, "dp", "tensor"),
        ),
        out_specs=(
            P("dp", "tensor"),
            P("dp", "tensor"),
            P(None, "tensor", "dp"),
            P(None, "tensor", "dp"),
            P(None, "dp", "tensor"),
        ),
        check_vma=False,
    )
```

```python
import functools

import jax
import jax.numpy as jnp
from jax import lax
from jax.experimental import pallas as pl
from jax.experimental.pallas import tpu as pltpu
from jax.sharding import PartitionSpec as P

BF16 = jnp.bfloat16
F32 = jnp.float32
I32 = jnp.int32
LANES = 128
VMEM = pl.BlockSpec(memory_space=pltpu.VMEM)
SMEM = pl.BlockSpec(memory_space=pltpu.SMEM)
HBM = pl.BlockSpec(memory_space=pltpu.HBM)


def dp_parts(n):
    z = n // 4
    z_lo = 4 if z >= 16 else 2
    return z // z_lo, z_lo


def near_members(n_zh, n_zl):
    return [((a + 1) % n_zl, x) for x in range(2) for a in range(n_zl)]


def far_members(n_zh, n_zl):
    return [(a + n_zh // 2) % n_zh for a in range(n_zh)]


def groups_of(n_zh, n_zl):
    near = [
        [((h * n_zl + low) * 2 + x) * 2 + c for low, x in near_members(n_zh, n_zl)]
        for h in range(n_zh)
        for c in range(2)
    ]
    far = [
        [((h * n_zl + low) * 2 + x) * 2 + c for h in far_members(n_zh, n_zl)]
        for low in range(n_zl)
        for x in range(2)
        for c in range(2)
    ]
    return near, far


def iota(shape, dim):
    return lax.broadcasted_iota(I32, shape, dim)


def dot(left, right, dims=((1,), (0,))):
    return lax.dot_general(left, right, (dims, ((), ())), preferred_element_type=F32)


def partial_kernel(tok_hbm, cot_hbm, count_hbm, gate_hbm, up_hbm, down_hbm, out_ref, tok, cot, count_ref, gate, up, down, both, one, sems):
    pairs = (
        (tok_hbm, tok),
        (gate_hbm, gate),
        (up_hbm, up),
        (cot_hbm, cot),
        (down_hbm, down),
        (count_hbm, count_ref),
    )
    copies = [pltpu.make_async_copy(src, dst, sems.at[k]) for k, (src, dst) in enumerate(pairs)]
    for copy in copies:
        copy.start()
    one[...] = jnp.zeros_like(one)
    total, features = tok.shape
    width = gate.shape[0]
    copies[5].wait()
    n_groups = count_ref.shape[1]
    spread = (iota((n_groups, total), 1) // 2 == iota((n_groups, total), 0)).astype(BF16)
    counts = jnp.broadcast_to(count_ref[...].astype(F32), (8, n_groups)).astype(BF16)
    limit = dot(counts, spread)[0:1, :]
    is_text = (iota((1, total), 1) % 2).astype(F32) < limit
    n, _, lanes = both.shape
    for j, (left, weight, needs) in enumerate(
        ((tok, gate, (0, 1)), (tok, up, (2,)), (cot, down, (3, 4)))
    ):
        for k in needs:
            copies[k].wait()
        rows = weight[...].reshape(2 * width, features)
        products = dot(rows, left[...], ((1,), (1,)))
        for c in range(n):
            here = slice(c * lanes, (c + 1) * lanes)
            both[c] = products[:, here]
            text = both[c, pl.ds(0, width, 2), :]
            image = both[c, pl.ds(1, width, 2), :]
            one[0:width, here] = jnp.where(is_text[:, here], text, image)
        out_ref[:, j * LANES : (j + 1) * LANES] = one[...].T


def rows_kernel(share_ref, out_ref):
    share = share_ref[0]
    for k in range(1, share_ref.shape[0]):
        share = share + share_ref[k]
    gate = share[:, :LANES]
    up = share[:, LANES : 2 * LANES]
    grad_hidden = share[:, 2 * LANES :]
    sig = jax.nn.sigmoid(gate)
    act = gate * sig
    hidden = (act * up).astype(BF16)
    grad_gate = (grad_hidden * up * sig * (1.0 + gate * (1.0 - sig))).astype(BF16)
    grad_up = (grad_hidden * act).astype(BF16)
    for k in range(out_ref.shape[0]):
        out_ref[k, :, :LANES] = hidden
        out_ref[k, :, LANES : 2 * LANES] = grad_gate
        out_ref[k, :, 2 * LANES :] = grad_up


def interleaved(rows, is_text, width):
    n = rows.shape[0]
    expand = (iota((LANES, 2 * width), 1) // 2 == iota((LANES, 2 * width), 0)).astype(BF16)
    wide = dot(rows, expand)
    is_even = iota((n, 2 * width), 1) % 2 == 0
    return jnp.where(is_even == is_text, wide, 0.0).astype(BF16)


def text_column(row, count_ref):
    n, n_groups = row.shape[0], count_ref.shape[1]
    hit = iota((n, n_groups), 1) == row // 2
    limit = jnp.sum(
        jnp.where(hit, count_ref[...].astype(F32), 0.0), axis=1, keepdims=True
    )
    return (row % 2).astype(F32) < limit


def half_sums(n_zh, n_zl, core, rows_ref, count_ref, gate, up, down):
    total = rows_ref.shape[0]
    width, _, features = gate.shape
    half = total // 2
    i = iota((half, 1), 0)
    d = i // (2 * n_zh)
    far = i % (2 * n_zh) // 2
    low = (d % n_zl + 1) % n_zl
    high = (far + n_zh // 2) % n_zh
    row = ((high * n_zl + low) * 2 + d // n_zl) * 4 + core * 2 + i % 2
    is_text = text_column(row, count_ref)
    pick = (iota((half, total), 1) == row).astype(BF16)
    rows = dot(pick, rows_ref[...]).astype(BF16)

    def wide(j):
        return interleaved(rows[:, j * LANES : (j + 1) * LANES], is_text, width)

    def flat(weight):
        return weight.reshape(2 * width, features)

    mixed = dot(wide(0), flat(down))
    grad = dot(wide(1), flat(gate)) + dot(wide(2), flat(up))
    return mixed, grad


def core_sums_kernel(n_zh, n_zl, side_ref, rows_ref, count_ref, gate_ref, up_ref, down_ref, out_ref):
    features = gate_ref.shape[2]
    mixed, grad = half_sums(
        n_zh, n_zl, side_ref[0], rows_ref, count_ref, gate_ref[...], up_ref[...], down_ref[...]
    )
    out_ref[:, :features] = mixed.astype(out_ref.dtype)
    out_ref[:, features:] = grad.astype(out_ref.dtype)


def add_kernel(keep_ref, got_ref, out_ref):
    out_ref[...] = (keep_ref[...] + got_ref[...].astype(F32)).astype(BF16)


def weight_grads_kernel(rows_ref, count_ref, tok_ref, cot_ref, gate_ref, up_ref, down_ref):
    total, features = tok_ref.shape
    width = gate_ref.shape[0]
    is_text = text_column(iota((total, 1), 0), count_ref)
    for j, (left, out) in enumerate(
        ((cot_ref, down_ref), (tok_ref, gate_ref), (tok_ref, up_ref))
    ):
        wide = interleaved(rows_ref[:, j * LANES : (j + 1) * LANES], is_text, width)
        out[...] = dot(wide, left[...], ((0,), (0,))).reshape(width, 2, features)


def program(n_zh, n_zl, n_tensor):
    near, far = groups_of(n_zh, n_zl)
    n_near = 2 * n_zl

    def on_device(tokens, cotangent, text_count, w_gate, w_up, w_down):
        total, features = tokens.shape
        width = w_gate.shape[2]
        half = total // 2
        lanes = min(total, LANES)
        counts = text_count.reshape(1, -1)
        gate_w = jnp.transpose(w_gate, (2, 0, 1))
        up_w = jnp.transpose(w_up, (2, 0, 1))
        down_w = jnp.transpose(w_down, (1, 0, 2))
        params = pltpu.CompilerParams(vmem_limit_bytes=24 * 1024 * 1024)
        n_dp = 4 * n_zh * n_zl
        pairs = [(i, i ^ 1) for i in range(n_dp)]
        in_hbm = [
            pltpu.with_memory_space_constraint(x, pltpu.HBM)
            for x in (tokens, cotangent, counts, gate_w, up_w, down_w)
        ]
        partial = pl.pallas_call(
            partial_kernel,
            out_shape=jax.ShapeDtypeStruct((total, 3 * LANES), F32),
            in_specs=[HBM] * 6,
            out_specs=VMEM,
            scratch_shapes=[
                pltpu.VMEM((total, features), BF16),
                pltpu.VMEM((total, features), BF16),
                pltpu.VMEM(counts.shape, I32),
                pltpu.VMEM((width, 2, features), BF16),
                pltpu.VMEM((width, 2, features), BF16),
                pltpu.VMEM((width, 2, features), BF16),
                pltpu.VMEM((total // lanes, 2 * width, lanes), F32),
                pltpu.VMEM((LANES, total), F32),
                pltpu.SemaphoreType.DMA((6,)),
            ],
            compiler_params=params,
            name="partial_sums",
        )(*in_hbm)
        partial = partial.reshape(n_tensor, total // n_tensor, 3 * LANES)
        shares = lax.all_to_all(partial, "tensor", 0, 0)
        copies = pl.pallas_call(
            rows_kernel,
            out_shape=jax.ShapeDtypeStruct(shares.shape, BF16),
            in_specs=[VMEM],
            out_specs=VMEM,
            compiler_params=params,
            name="hidden_rows",
        )(shares)
        rows = lax.all_to_all(copies, "tensor", 0, 0).reshape(total, 3 * LANES)

        core = (lax.axis_index("dp") % 2).astype(I32).reshape(1)

        def core_sums(side, dtype):
            return pl.pallas_call(
                functools.partial(core_sums_kernel, n_zh, n_zl),
                out_shape=jax.ShapeDtypeStruct((half, 2 * features), dtype),
                in_specs=[SMEM] + [VMEM] * 5,
                out_specs=VMEM,
                compiler_params=params,
                cost_estimate=pl.CostEstimate(
                    flops=12 * half * width * features, bytes_accessed=4 << 20, transcendentals=0
                ),
                name="core_token_sums",
            )(side, rows, counts, gate_w, up_w, down_w)

        got = lax.ppermute(core_sums(1 - core, BF16), "dp", pairs)
        chip = pl.pallas_call(
            add_kernel,
            out_shape=jax.ShapeDtypeStruct((half, 2 * features), BF16),
            in_specs=[VMEM] * 2,
            out_specs=VMEM,
            compiler_params=params,
            name="chip_sums",
        )(core_sums(core, F32), got)
        chip = chip.reshape(n_near, half // n_near, 2 * features)
        parts = lax.all_to_all(chip, "dp", 0, 0, axis_index_groups=near)
        grads = pl.pallas_call(
            weight_grads_kernel,
            out_shape=(jax.ShapeDtypeStruct((width, 2, features), F32),) * 3,
            in_specs=[VMEM] * 4,
            out_specs=(VMEM,) * 3,
            compiler_params=params,
            cost_estimate=pl.CostEstimate(
                flops=12 * total * width * features, bytes_accessed=4 << 20, transcendentals=0
            ),
            name="weight_grads",
        )(rows, counts, tokens, cotangent)
        mine = jnp.sum(parts.astype(F32), axis=0).astype(BF16)
        mine = mine.reshape(n_zh, 2, 2 * features)
        mine, gate_g, up_g, down_g = lax.optimization_barrier((mine,) + tuple(grads))
        parts = lax.all_to_all(mine, "dp", 0, 0, axis_index_groups=far)
        out = jnp.sum(parts.astype(F32), axis=0).astype(BF16)
        return (
            out[:, :features],
            out[:, features:],
            jnp.transpose(gate_g, (1, 2, 0)),
            jnp.transpose(up_g, (1, 2, 0)),
            jnp.transpose(down_g, (1, 0, 2)),
        )

    return on_device


def solution(mesh):
    n_zh, n_zl = dp_parts(mesh.shape["dp"])
    return jax.shard_map(
        program(n_zh, n_zl, mesh.shape["tensor"]),
        mesh=mesh,
        in_specs=(
            P(None, "tensor"),
            P(None, "tensor"),
            P(),
            P(None, "tensor", "dp"),
            P(None, "tensor", "dp"),
            P(None, "dp", "tensor"),
        ),
        out_specs=(
            P("dp", "tensor"),
            P("dp", "tensor"),
            P(None, "tensor", "dp"),
            P(None, "tensor", "dp"),
            P(None, "dp", "tensor"),
        ),
        check_vma=False,
    )
```

```python
import functools

import jax
import jax.numpy as jnp
from jax import lax
from jax.experimental import pallas as pl
from jax.experimental.pallas import tpu as pltpu
from jax.sharding import PartitionSpec as P

BF16 = jnp.bfloat16
F32 = jnp.float32
I32 = jnp.int32
LANES = 128
VMEM = pl.BlockSpec(memory_space=pltpu.VMEM)
SMEM = pl.BlockSpec(memory_space=pltpu.SMEM)
HBM = pl.BlockSpec(memory_space=pltpu.HBM)


def dp_parts(n):
    z = n // 4
    z_lo = 4 if z >= 16 else 2
    return z // z_lo, z_lo


def near_members(n_zh, n_zl):
    return [((a + 1) % n_zl, x) for x in range(2) for a in range(n_zl)]


def far_members(n_zh, n_zl):
    return [(a + n_zh // 2) % n_zh for a in range(n_zh)]


def groups_of(n_zh, n_zl):
    near = [
        [((h * n_zl + low) * 2 + x) * 2 + c for low, x in near_members(n_zh, n_zl)]
        for h in range(n_zh)
        for c in range(2)
    ]
    far = [
        [((h * n_zl + low) * 2 + x) * 2 + c for h in far_members(n_zh, n_zl)]
        for low in range(n_zl)
        for x in range(2)
        for c in range(2)
    ]
    return near, far


def iota(shape, dim):
    return lax.broadcasted_iota(I32, shape, dim)


def dot(left, right, dims=((1,), (0,))):
    return lax.dot_general(left, right, (dims, ((), ())), preferred_element_type=F32)


def per_share(width, n):
    return -(-width // n)


def packed_rows(width, n, chunks):
    return -(-3 * chunks * per_share(width, n) // 8) * 8


def partial_kernel(core_ref, tok_hbm, cot_hbm, count_hbm, gate_hbm, up_hbm, down_hbm, out_ref, tok, cot, count_ref, gate, up, down, both, sems):
    pairs = (
        (tok_hbm, tok),
        (gate_hbm, gate),
        (up_hbm, up),
        (cot_hbm, cot),
        (down_hbm, down),
        (count_hbm, count_ref),
    )
    copies = [pltpu.make_async_copy(src, dst, sems.at[k]) for k, (src, dst) in enumerate(pairs)]
    for copy in copies:
        copy.start()
    total, features = tok.shape
    width = gate.shape[0]
    shares = out_ref.shape[0]
    part = per_share(width, shares)
    chunks, depth, lanes = both.shape
    out_ref[...] = jnp.zeros_like(out_ref)
    both[...] = jnp.zeros_like(both)
    copies[5].wait()
    is_text = text_lanes(count_ref, total)
    for w, (left, weight, needs) in enumerate(
        ((tok, gate, (0, 1)), (tok, up, (2,)), (cot, down, (3, 4)))
    ):
        for k in needs:
            copies[k].wait()
        rows = weight[...].reshape(2 * width, features)
        products = dot(rows, left[...], ((1,), (1,)))
        for c in range(chunks):
            here = slice(c * lanes, (c + 1) * lanes)
            both[c, 0 : 2 * width, :] = products[:, here]
            at = (3 * c + w) * part
            for share in range(shares):
                text = both[c, pl.ds(2 * share, part, 2 * shares), :]
                image = both[c, pl.ds(2 * share + 1, part, 2 * shares), :]
                out_ref[share, at : at + part, :] = jnp.where(is_text[:, here], text, image)


def rows_kernel(width, share_ref, out_ref):
    shares, depth, _ = share_ref.shape
    part = per_share(width, shares)
    chunks = depth // (3 * part)
    total = share_ref[0]
    for k in range(1, shares):
        total = total + share_ref[k]
    pieces = []
    for c in range(chunks):
        at = 3 * c * part
        gate = total[at : at + part]
        up = total[at + part : at + 2 * part]
        grad_hidden = total[at + 2 * part : at + 3 * part]
        sig = jax.nn.sigmoid(gate)
        act = gate * sig
        pieces += [
            act * up,
            grad_hidden * up * sig * (1.0 + gate * (1.0 - sig)),
            grad_hidden * act,
        ]
    pad = depth - 3 * chunks * part
    if pad:
        pieces.append(jnp.zeros((pad, total.shape[1]), F32))
    rows = jnp.concatenate(pieces, axis=0).astype(BF16)
    for k in range(shares):
        out_ref[k] = rows


def unpacked(width, rows_ref, w):
    shares, depth, lanes = rows_ref.shape
    part = per_share(width, shares)
    chunks = depth // (3 * part)
    rows = rows_ref[...].reshape(shares * depth, lanes)
    unit = iota((2 * width, shares * depth), 0) // 2
    column = iota((2 * width, shares * depth), 1) - unit % shares * depth - unit // shares
    wide = [
        dot((column == (3 * c + w) * part).astype(BF16), rows) for c in range(chunks)
    ]
    return jnp.concatenate(wide, axis=1) if chunks > 1 else wide[0]


def text_lanes(count_ref, total):
    n_groups = count_ref.shape[1]
    spread = (iota((n_groups, total), 1) // 2 == iota((n_groups, total), 0)).astype(BF16)
    counts = jnp.broadcast_to(count_ref[...].astype(F32), (8, n_groups)).astype(BF16)
    limit = dot(counts, spread)[0:1, :]
    return (iota((1, total), 1) % 2).astype(F32) < limit


def text_column(row, count_ref):
    n, n_groups = row.shape[0], count_ref.shape[1]
    hit = iota((n, n_groups), 1) == row // 2
    limit = jnp.sum(
        jnp.where(hit, count_ref[...].astype(F32), 0.0), axis=1, keepdims=True
    )
    return (row % 2).astype(F32) < limit


def half_sums(n_zh, n_zl, side, wide, count_ref, gate_ref, up_ref, down_ref, out_ref):
    width, _, features = gate_ref.shape
    total = wide[0].shape[1]
    half = total // 2
    i = iota((half, 1), 0)
    d = i // (2 * n_zh)
    far = i % (2 * n_zh) // 2
    low = (d % n_zl + 1) % n_zl
    high = (far + n_zh // 2) % n_zh
    row = ((high * n_zl + low) * 2 + d // n_zl) * 4 + side * 2 + i % 2
    is_text = text_column(row, count_ref)
    is_mine = (iota((half, 2 * width), 1) % 2 == 0) == is_text
    pick = (iota((half, total), 1) == row).astype(BF16)

    def product(w, weight):
        left = jnp.where(is_mine, dot(pick, wide[w], ((1,), (1,))), 0.0).astype(BF16)
        return dot(left, weight[...].reshape(2 * width, features))

    out_ref[:, :features] = product(0, down_ref).astype(out_ref.dtype)
    out_ref[:, features:] = (product(1, gate_ref) + product(2, up_ref)).astype(out_ref.dtype)


def send_sums_kernel(n_zh, n_zl, core_ref, rows_ref, count_ref, gate_ref, up_ref, down_ref, out_ref, wide_ref):
    width = gate_ref.shape[0]
    wide = [unpacked(width, rows_ref, w).astype(BF16) for w in range(3)]
    half_sums(
        n_zh, n_zl, 1 - core_ref[0], wide, count_ref, gate_ref, up_ref, down_ref, out_ref
    )
    for w in range(3):
        wide_ref[w] = wide[w]


def keep_sums_kernel(n_zh, n_zl, core_ref, wide_ref, count_ref, gate_ref, up_ref, down_ref, out_ref):
    wide = [wide_ref[w] for w in range(3)]
    half_sums(n_zh, n_zl, core_ref[0], wide, count_ref, gate_ref, up_ref, down_ref, out_ref)


def add_kernel(keep_ref, got_ref, out_ref):
    out_ref[...] = (keep_ref[...] + got_ref[...].astype(F32)).astype(BF16)


def weight_grads_kernel(wide_ref, count_ref, tok_ref, cot_ref, gate_ref, up_ref, down_ref):
    total, features = tok_ref.shape
    width = gate_ref.shape[0]
    is_text = text_lanes(count_ref, total)
    is_mine = (iota((2 * width, total), 0) % 2 == 0) == is_text
    for w, (left, out) in enumerate(((cot_ref, down_ref), (tok_ref, gate_ref), (tok_ref, up_ref))):
        rows = jnp.where(is_mine, wide_ref[w].astype(F32), 0.0).astype(BF16)
        out[...] = dot(rows, left[...]).reshape(width, 2, features)


def program(n_zh, n_zl, n_tensor):
    near, far = groups_of(n_zh, n_zl)
    n_near = 2 * n_zl

    def on_device(tokens, cotangent, text_count, w_gate, w_up, w_down):
        total, features = tokens.shape
        width = w_gate.shape[2]
        half = total // 2
        lanes = min(total, LANES)
        counts = text_count.reshape(1, -1)
        gate_w = jnp.transpose(w_gate, (2, 0, 1))
        up_w = jnp.transpose(w_up, (2, 0, 1))
        down_w = jnp.transpose(w_down, (1, 0, 2))
        core = (lax.axis_index("dp") % 2).astype(I32).reshape(1)
        params = pltpu.CompilerParams(vmem_limit_bytes=24 * 1024 * 1024)
        n_dp = 4 * n_zh * n_zl
        pairs = [(i, i ^ 1) for i in range(n_dp)]
        in_hbm = [
            pltpu.with_memory_space_constraint(x, pltpu.HBM)
            for x in (tokens, cotangent, counts, gate_w, up_w, down_w)
        ]
        chunks = total // lanes
        depth = packed_rows(width, n_tensor, chunks)
        partial = pl.pallas_call(
            partial_kernel,
            out_shape=jax.ShapeDtypeStruct((n_tensor, depth, lanes), F32),
            in_specs=[SMEM] + [HBM] * 6,
            out_specs=VMEM,
            scratch_shapes=[
                pltpu.VMEM((total, features), BF16),
                pltpu.VMEM((total, features), BF16),
                pltpu.VMEM(counts.shape, I32),
                pltpu.VMEM((width, 2, features), BF16),
                pltpu.VMEM((width, 2, features), BF16),
                pltpu.VMEM((width, 2, features), BF16),
                pltpu.VMEM((chunks, 2 * n_tensor * per_share(width, n_tensor), lanes), F32),
                pltpu.SemaphoreType.DMA((6,)),
            ],
            compiler_params=params,
            name="partial_sums",
        )(core, *in_hbm)
        shares = lax.all_to_all(partial, "tensor", 0, 0)
        copies = pl.pallas_call(
            functools.partial(rows_kernel, width),
            out_shape=jax.ShapeDtypeStruct(shares.shape, BF16),
            in_specs=[VMEM],
            out_specs=VMEM,
            compiler_params=params,
            name="hidden_rows",
        )(shares)
        rows = lax.all_to_all(copies, "tensor", 0, 0)

        cost = pl.CostEstimate(
            flops=12 * half * width * features, bytes_accessed=4 << 20, transcendentals=0
        )
        send, wide = pl.pallas_call(
            functools.partial(send_sums_kernel, n_zh, n_zl),
            out_shape=(
                jax.ShapeDtypeStruct((half, 2 * features), BF16),
                jax.ShapeDtypeStruct((3, 2 * width, total), BF16),
            ),
            in_specs=[SMEM] + [VMEM] * 5,
            out_specs=(VMEM, VMEM),
            compiler_params=params,
            cost_estimate=cost,
            name="other_core_sums",
        )(core, rows, counts, gate_w, up_w, down_w)
        keep = pl.pallas_call(
            functools.partial(keep_sums_kernel, n_zh, n_zl),
            out_shape=jax.ShapeDtypeStruct((half, 2 * features), F32),
            in_specs=[SMEM] + [VMEM] * 5,
            out_specs=VMEM,
            compiler_params=params,
            cost_estimate=cost,
            name="own_core_sums",
        )(core, wide, counts, gate_w, up_w, down_w)
        got = lax.ppermute(send, "dp", pairs)
        chip = pl.pallas_call(
            add_kernel,
            out_shape=jax.ShapeDtypeStruct((half, 2 * features), BF16),
            in_specs=[VMEM] * 2,
            out_specs=VMEM,
            compiler_params=params,
            name="chip_sums",
        )(keep, got)
        chip = chip.reshape(n_near, half // n_near, 2 * features)
        parts = lax.all_to_all(chip, "dp", 0, 0, axis_index_groups=near)
        grads = pl.pallas_call(
            weight_grads_kernel,
            out_shape=(jax.ShapeDtypeStruct((width, 2, features), F32),) * 3,
            in_specs=[VMEM] * 4,
            out_specs=(VMEM,) * 3,
            compiler_params=params,
            cost_estimate=pl.CostEstimate(
                flops=12 * total * width * features, bytes_accessed=4 << 20, transcendentals=0
            ),
            name="weight_grads",
        )(wide, counts, tokens, cotangent)
        mine = jnp.sum(parts.astype(F32), axis=0).astype(BF16)
        mine = mine.reshape(n_zh, 2, 2 * features)
        mine, gate_g, up_g, down_g = lax.optimization_barrier((mine,) + tuple(grads))
        parts = lax.all_to_all(mine, "dp", 0, 0, axis_index_groups=far)
        out = jnp.sum(parts.astype(F32), axis=0).astype(BF16)
        return (
            out[:, :features],
            out[:, features:],
            jnp.transpose(gate_g, (1, 2, 0)),
            jnp.transpose(up_g, (1, 2, 0)),
            jnp.transpose(down_g, (1, 0, 2)),
        )

    return on_device


def solution(mesh):
    n_zh, n_zl = dp_parts(mesh.shape["dp"])
    return jax.shard_map(
        program(n_zh, n_zl, mesh.shape["tensor"]),
        mesh=mesh,
        in_specs=(
            P(None, "tensor"),
            P(None, "tensor"),
            P(),
            P(None, "tensor", "dp"),
            P(None, "tensor", "dp"),
            P(None, "dp", "tensor"),
        ),
        out_specs=(
            P("dp", "tensor"),
            P("dp", "tensor"),
            P(None, "tensor", "dp"),
            P(None, "tensor", "dp"),
            P(None, "dp", "tensor"),
        ),
        check_vma=False,
    )
```

```python
import functools

import jax
import jax.numpy as jnp
from jax import lax
from jax.experimental import pallas as pl
from jax.experimental.pallas import tpu as pltpu
from jax.sharding import PartitionSpec as P

BF16 = jnp.bfloat16
F32 = jnp.float32
I32 = jnp.int32
LANES = 128
VMEM = pl.BlockSpec(memory_space=pltpu.VMEM)
SMEM = pl.BlockSpec(memory_space=pltpu.SMEM)
HBM = pl.BlockSpec(memory_space=pltpu.HBM)


def dp_parts(n):
    z = n // 4
    z_lo = 4 if z >= 16 else 2
    return z // z_lo, z_lo


def low_order(n_zl):
    return sorted(range(n_zl), key=lambda low: (abs(low - n_zl // 2), low))


def high_order(n_zh):
    return sorted(range(n_zh), key=lambda h: (h != n_zh // 2, min(h, n_zh - h), h))


def at_place(order, place):
    value = jnp.zeros_like(place)
    for k, entry in enumerate(order):
        value = jnp.where(place == k, entry, value)
    return value


def groups_of(n_zh, n_zl):
    near = [
        [((h * n_zl + low) * 2 + x) * 2 + c for x in range(2) for low in low_order(n_zl)]
        for h in range(n_zh)
        for c in range(2)
    ]
    far = [
        [((h * n_zl + low) * 2 + x) * 2 + c for h in high_order(n_zh)]
        for low in range(n_zl)
        for x in range(2)
        for c in range(2)
    ]
    return near, far


def iota(shape, dim):
    return lax.broadcasted_iota(I32, shape, dim)


def dot(left, right, dims=((1,), (0,))):
    return lax.dot_general(left, right, (dims, ((), ())), preferred_element_type=F32)


def per_share(width, n):
    return -(-width // n)


def packed_rows(width, n, chunks):
    return -(-3 * chunks * per_share(width, n) // 8) * 8


def partial_kernel(core_ref, tok_hbm, cot_hbm, count_hbm, gate_hbm, up_hbm, down_hbm, out_ref, tok, cot, count_ref, gate, up, down, both, sems):
    pairs = (
        (tok_hbm, tok),
        (gate_hbm, gate),
        (up_hbm, up),
        (cot_hbm, cot),
        (down_hbm, down),
        (count_hbm, count_ref),
    )
    copies = [pltpu.make_async_copy(src, dst, sems.at[k]) for k, (src, dst) in enumerate(pairs)]
    for copy in copies:
        copy.start()
    total, features = tok.shape
    width = gate.shape[0]
    shares = out_ref.shape[0]
    part = per_share(width, shares)
    chunks, depth, lanes = both.shape
    out_ref[...] = jnp.zeros_like(out_ref)
    both[...] = jnp.zeros_like(both)
    copies[5].wait()
    is_text = text_lanes(count_ref, total)
    for w, (left, weight, needs) in enumerate(
        ((tok, gate, (0, 1)), (tok, up, (2,)), (cot, down, (3, 4)))
    ):
        for k in needs:
            copies[k].wait()
        rows = weight[...].reshape(2 * width, features)
        products = dot(rows, left[...], ((1,), (1,)))
        for c in range(chunks):
            here = slice(c * lanes, (c + 1) * lanes)
            both[c, 0 : 2 * width, :] = products[:, here]
            at = (3 * c + w) * part
            for share in range(shares):
                text = both[c, pl.ds(2 * share, part, 2 * shares), :]
                image = both[c, pl.ds(2 * share + 1, part, 2 * shares), :]
                out_ref[share, at : at + part, :] = jnp.where(is_text[:, here], text, image)


def rows_kernel(width, share_ref, out_ref):
    shares, depth, _ = share_ref.shape
    part = per_share(width, shares)
    chunks = depth // (3 * part)
    total = share_ref[0]
    for k in range(1, shares):
        total = total + share_ref[k]
    pieces = []
    for c in range(chunks):
        at = 3 * c * part
        gate = total[at : at + part]
        up = total[at + part : at + 2 * part]
        grad_hidden = total[at + 2 * part : at + 3 * part]
        sig = jax.nn.sigmoid(gate)
        act = gate * sig
        pieces += [
            act * up,
            grad_hidden * up * sig * (1.0 + gate * (1.0 - sig)),
            grad_hidden * act,
        ]
    pad = depth - 3 * chunks * part
    if pad:
        pieces.append(jnp.zeros((pad, total.shape[1]), F32))
    rows = jnp.concatenate(pieces, axis=0).astype(BF16)
    for k in range(shares):
        out_ref[k] = rows


def unpacked(width, rows_ref):
    shares, depth, lanes = rows_ref.shape
    part = per_share(width, shares)
    room = -(-part // 16) * 16
    chunks = depth // (3 * part)
    unit = iota((2 * width, shares * room), 0) // 2
    column = iota((2 * width, shares * room), 1)
    move = (column == unit % shares * room + unit // shares).astype(BF16)
    rows = rows_ref[...].astype(F32)
    pad = jnp.zeros((shares, room - part, lanes), F32)

    def piece(c, w):
        at = (3 * c + w) * part
        some = jnp.concatenate((rows[:, at : at + part], pad), axis=1)
        return dot(move, some.reshape(shares * room, lanes).astype(BF16)).astype(BF16)

    return [jnp.concatenate([piece(c, w) for c in range(chunks)], axis=1) for w in range(3)]


def text_lanes(count_ref, total):
    n_groups = count_ref.shape[1]
    spread = (iota((n_groups, total), 1) // 2 == iota((n_groups, total), 0)).astype(BF16)
    counts = jnp.broadcast_to(count_ref[...].astype(F32), (8, n_groups)).astype(BF16)
    limit = dot(counts, spread)[0:1, :]
    return (iota((1, total), 1) % 2).astype(F32) < limit


def text_column(row, count_ref):
    n, n_groups = row.shape[0], count_ref.shape[1]
    hit = iota((n, n_groups), 1) == row // 2
    limit = jnp.sum(
        jnp.where(hit, count_ref[...].astype(F32), 0.0), axis=1, keepdims=True
    )
    return (row % 2).astype(F32) < limit


def half_sums(n_zh, n_zl, side, wide, count_ref, gate_ref, up_ref, down_ref, out_ref):
    width, _, features = gate_ref.shape
    total = wide[0].shape[1]
    half = total // 2
    i = iota((half, 1), 0)
    d = i // (2 * n_zh)
    far = i % (2 * n_zh) // 2
    low = at_place(low_order(n_zl), d % n_zl)
    high = at_place(high_order(n_zh), far)
    row = ((high * n_zl + low) * 2 + d // n_zl) * 4 + side * 2 + i % 2
    is_text = text_column(row, count_ref)
    is_mine = (iota((half, 2 * width), 1) % 2 == 0) == is_text
    pick = (iota((half, total), 1) == row).astype(BF16)

    def product(w, weight):
        left = jnp.where(is_mine, dot(pick, wide[w], ((1,), (1,))), 0.0).astype(BF16)
        return dot(left, weight[...].reshape(2 * width, features))

    out_ref[:, :features] = product(0, down_ref).astype(out_ref.dtype)
    out_ref[:, features:] = (product(1, gate_ref) + product(2, up_ref)).astype(out_ref.dtype)


def send_sums_kernel(n_zh, n_zl, core_ref, rows_ref, count_ref, gate_ref, up_ref, down_ref, out_ref, wide_ref):
    width = gate_ref.shape[0]
    wide = unpacked(width, rows_ref)
    half_sums(
        n_zh, n_zl, 1 - core_ref[0], wide, count_ref, gate_ref, up_ref, down_ref, out_ref
    )
    for w in range(3):
        wide_ref[w] = wide[w]


def keep_sums_kernel(n_zh, n_zl, core_ref, wide_ref, count_ref, gate_ref, up_ref, down_ref, out_ref):
    wide = [wide_ref[w] for w in range(3)]
    half_sums(n_zh, n_zl, core_ref[0], wide, count_ref, gate_ref, up_ref, down_ref, out_ref)


def add_kernel(keep_ref, got_ref, out_ref):
    out_ref[...] = (keep_ref[...] + got_ref[...].astype(F32)).astype(BF16)


def weight_grads_kernel(wide_ref, count_ref, tok_ref, cot_ref, gate_ref, up_ref, down_ref):
    total, features = tok_ref.shape
    width = gate_ref.shape[0]
    is_text = text_lanes(count_ref, total)
    is_mine = (iota((2 * width, total), 0) % 2 == 0) == is_text
    for w, (left, out) in enumerate(((cot_ref, down_ref), (tok_ref, gate_ref), (tok_ref, up_ref))):
        rows = jnp.where(is_mine, wide_ref[w].astype(F32), 0.0).astype(BF16)
        out[...] = dot(rows, left[...]).reshape(width, 2, features)


def program(n_zh, n_zl, n_tensor):
    near, far = groups_of(n_zh, n_zl)
    n_near = 2 * n_zl

    def on_device(tokens, cotangent, text_count, w_gate, w_up, w_down):
        total, features = tokens.shape
        width = w_gate.shape[2]
        half = total // 2
        lanes = min(total, LANES)
        counts = text_count.reshape(1, -1)
        gate_w = jnp.transpose(w_gate, (2, 0, 1))
        up_w = jnp.transpose(w_up, (2, 0, 1))
        down_w = jnp.transpose(w_down, (1, 0, 2))
        core = (lax.axis_index("dp") % 2).astype(I32).reshape(1)
        params = pltpu.CompilerParams(vmem_limit_bytes=24 * 1024 * 1024)
        n_dp = 4 * n_zh * n_zl
        pairs = [(i, i ^ 1) for i in range(n_dp)]
        in_hbm = [
            pltpu.with_memory_space_constraint(x, pltpu.HBM)
            for x in (tokens, cotangent, counts, gate_w, up_w, down_w)
        ]
        chunks = total // lanes
        depth = packed_rows(width, n_tensor, chunks)
        partial = pl.pallas_call(
            partial_kernel,
            out_shape=jax.ShapeDtypeStruct((n_tensor, depth, lanes), F32),
            in_specs=[SMEM] + [HBM] * 6,
            out_specs=VMEM,
            scratch_shapes=[
                pltpu.VMEM((total, features), BF16),
                pltpu.VMEM((total, features), BF16),
                pltpu.VMEM(counts.shape, I32),
                pltpu.VMEM((width, 2, features), BF16),
                pltpu.VMEM((width, 2, features), BF16),
                pltpu.VMEM((width, 2, features), BF16),
                pltpu.VMEM((chunks, 2 * n_tensor * per_share(width, n_tensor), lanes), F32),
                pltpu.SemaphoreType.DMA((6,)),
            ],
            compiler_params=params,
            name="partial_sums",
        )(core, *in_hbm)
        shares = lax.all_to_all(partial, "tensor", 0, 0)
        copies = pl.pallas_call(
            functools.partial(rows_kernel, width),
            out_shape=jax.ShapeDtypeStruct(shares.shape, BF16),
            in_specs=[VMEM],
            out_specs=VMEM,
            compiler_params=params,
            name="hidden_rows",
        )(shares)
        rows = lax.all_to_all(copies, "tensor", 0, 0)

        cost = pl.CostEstimate(
            flops=12 * half * width * features, bytes_accessed=4 << 20, transcendentals=0
        )
        send, wide = pl.pallas_call(
            functools.partial(send_sums_kernel, n_zh, n_zl),
            out_shape=(
                jax.ShapeDtypeStruct((half, 2 * features), BF16),
                jax.ShapeDtypeStruct((3, 2 * width, total), BF16),
            ),
            in_specs=[SMEM] + [VMEM] * 5,
            out_specs=(VMEM, VMEM),
            compiler_params=params,
            cost_estimate=cost,
            name="other_core_sums",
        )(core, rows, counts, gate_w, up_w, down_w)
        keep = pl.pallas_call(
            functools.partial(keep_sums_kernel, n_zh, n_zl),
            out_shape=jax.ShapeDtypeStruct((half, 2 * features), F32),
            in_specs=[SMEM] + [VMEM] * 5,
            out_specs=VMEM,
            compiler_params=params,
            cost_estimate=cost,
            name="own_core_sums",
        )(core, wide, counts, gate_w, up_w, down_w)
        got = lax.ppermute(send, "dp", pairs)
        chip = pl.pallas_call(
            add_kernel,
            out_shape=jax.ShapeDtypeStruct((half, 2 * features), BF16),
            in_specs=[VMEM] * 2,
            out_specs=VMEM,
            compiler_params=params,
            name="chip_sums",
        )(keep, got)
        chip = chip.reshape(n_near, half // n_near, 2 * features)
        parts = lax.all_to_all(chip, "dp", 0, 0, axis_index_groups=near)
        grads = pl.pallas_call(
            weight_grads_kernel,
            out_shape=(jax.ShapeDtypeStruct((width, 2, features), F32),) * 3,
            in_specs=[VMEM] * 4,
            out_specs=(VMEM,) * 3,
            compiler_params=params,
            cost_estimate=pl.CostEstimate(
                flops=12 * total * width * features, bytes_accessed=4 << 20, transcendentals=0
            ),
            name="weight_grads",
        )(wide, counts, tokens, cotangent)
        mine = jnp.sum(parts.astype(F32), axis=0).astype(BF16)
        mine = mine.reshape(n_zh, 2, 2 * features)
        mine, gate_g, up_g, down_g = lax.optimization_barrier((mine,) + tuple(grads))
        parts = lax.all_to_all(mine, "dp", 0, 0, axis_index_groups=far)
        out = jnp.sum(parts.astype(F32), axis=0).astype(BF16)
        return (
            out[:, :features],
            out[:, features:],
            jnp.transpose(gate_g, (1, 2, 0)),
            jnp.transpose(up_g, (1, 2, 0)),
            jnp.transpose(down_g, (1, 0, 2)),
        )

    return on_device


def solution(mesh):
    n_zh, n_zl = dp_parts(mesh.shape["dp"])
    return jax.shard_map(
        program(n_zh, n_zl, mesh.shape["tensor"]),
        mesh=mesh,
        in_specs=(
            P(None, "tensor"),
            P(None, "tensor"),
            P(),
            P(None, "tensor", "dp"),
            P(None, "tensor", "dp"),
            P(None, "dp", "tensor"),
        ),
        out_specs=(
            P("dp", "tensor"),
            P("dp", "tensor"),
            P(None, "tensor", "dp"),
            P(None, "tensor", "dp"),
            P(None, "dp", "tensor"),
        ),
        check_vma=False,
    )
```

```python
import functools

import jax
import jax.numpy as jnp
from jax import lax
from jax.experimental import pallas as pl
from jax.experimental.pallas import tpu as pltpu
from jax.sharding import PartitionSpec as P

BF16 = jnp.bfloat16
F32 = jnp.float32
I32 = jnp.int32
LANES = 128
VMEM = pl.BlockSpec(memory_space=pltpu.VMEM)
SMEM = pl.BlockSpec(memory_space=pltpu.SMEM)
HBM = pl.BlockSpec(memory_space=pltpu.HBM)


def dp_parts(n):
    z = n // 4
    z_lo = 4 if z >= 16 else 2
    return z // z_lo, z_lo


def low_order(n_zl):
    return sorted(range(n_zl), key=lambda low: (abs(low - n_zl // 2), low))


def high_order(n_zh):
    return sorted(range(n_zh), key=lambda h: (h != n_zh // 2, min(h, n_zh - h), h))


def at_place(order, place):
    value = jnp.zeros_like(place)
    for k, entry in enumerate(order):
        value = jnp.where(place == k, entry, value)
    return value


def groups_of(n_zh, n_zl):
    near = [
        [((h * n_zl + low) * 2 + x) * 2 + c for x in range(2) for low in low_order(n_zl)]
        for h in range(n_zh)
        for c in range(2)
    ]
    far = [
        [((h * n_zl + low) * 2 + x) * 2 + c for h in high_order(n_zh)]
        for low in range(n_zl)
        for x in range(2)
        for c in range(2)
    ]
    return near, far


def iota(shape, dim):
    return lax.broadcasted_iota(I32, shape, dim)


def dot(left, right, dims=((1,), (0,))):
    return lax.dot_general(left, right, (dims, ((), ())), preferred_element_type=F32)


def per_share(width, n):
    return -(-width // n)


def packed_rows(width, n, chunks):
    return -(-3 * chunks * per_share(width, n) // 8) * 8


def partial_kernel(core_ref, tok_hbm, cot_hbm, count_hbm, gate_hbm, up_hbm, down_hbm, out_ref, flat_ref, tok, cot, count_ref, gate, up, down, both, sems):
    pairs = (
        (count_hbm, count_ref),
        (tok_hbm, tok),
        (gate_hbm, gate),
        (up_hbm, up),
        (cot_hbm, cot),
        (down_hbm, down),
    )
    copies = [pltpu.make_async_copy(src, dst, sems.at[k]) for k, (src, dst) in enumerate(pairs)]
    for copy in copies:
        copy.start()
    total, features = tok.shape
    width = gate.shape[0]
    shares = out_ref.shape[0]
    part = per_share(width, shares)
    chunks, depth, lanes = both.shape
    out_ref[...] = jnp.zeros_like(out_ref)
    both[...] = jnp.zeros_like(both)
    copies[0].wait()
    is_text = text_lanes(count_ref, total)
    for w, (left, weight, needs) in enumerate(
        ((tok, gate, (1, 2)), (tok, up, (3,)), (cot, down, (4, 5)))
    ):
        for k in needs:
            copies[k].wait()
        rows = weight[...].reshape(2 * width, features)
        flat_ref[w] = rows
        products = dot(rows, left[...], ((1,), (1,)))
        for c in range(chunks):
            here = slice(c * lanes, (c + 1) * lanes)
            both[c, 0 : 2 * width, :] = products[:, here]
            at = (3 * c + w) * part
            for share in range(shares):
                text = both[c, pl.ds(2 * share, part, 2 * shares), :]
                image = both[c, pl.ds(2 * share + 1, part, 2 * shares), :]
                out_ref[share, at : at + part, :] = jnp.where(is_text[:, here], text, image)


def rows_kernel(width, share_ref, out_ref):
    shares, depth, _ = share_ref.shape
    part = per_share(width, shares)
    chunks = depth // (3 * part)
    total = share_ref[0]
    for k in range(1, shares):
        total = total + share_ref[k]
    pieces = []
    for c in range(chunks):
        at = 3 * c * part
        gate = total[at : at + part]
        up = total[at + part : at + 2 * part]
        grad_hidden = total[at + 2 * part : at + 3 * part]
        sig = jax.nn.sigmoid(gate)
        act = gate * sig
        pieces += [
            act * up,
            grad_hidden * up * sig * (1.0 + gate * (1.0 - sig)),
            grad_hidden * act,
        ]
    pad = depth - 3 * chunks * part
    if pad:
        pieces.append(jnp.zeros((pad, total.shape[1]), F32))
    rows = jnp.concatenate(pieces, axis=0).astype(BF16)
    for k in range(shares):
        out_ref[k] = rows


def unpacked(width, rows_ref):
    shares, depth, lanes = rows_ref.shape
    part = per_share(width, shares)
    room = -(-part // 16) * 16
    chunks = depth // (3 * part)
    unit = iota((2 * width, shares * room), 0) // 2
    column = iota((2 * width, shares * room), 1)
    move = (column == unit % shares * room + unit // shares).astype(BF16)
    rows = rows_ref[...].astype(F32)
    pad = jnp.zeros((shares, room - part, lanes), F32)

    def piece(c, w):
        at = (3 * c + w) * part
        some = jnp.concatenate((rows[:, at : at + part], pad), axis=1)
        return dot(move, some.reshape(shares * room, lanes).astype(BF16)).astype(BF16)

    return [jnp.concatenate([piece(c, w) for c in range(chunks)], axis=1) for w in range(3)]


def text_lanes(count_ref, total):
    n_groups = count_ref.shape[1]
    spread = (iota((n_groups, total), 1) // 2 == iota((n_groups, total), 0)).astype(BF16)
    counts = jnp.broadcast_to(count_ref[...].astype(F32), (8, n_groups)).astype(BF16)
    limit = dot(counts, spread)[0:1, :]
    return (iota((1, total), 1) % 2).astype(F32) < limit


def text_column(row, count_ref):
    n, n_groups = row.shape[0], count_ref.shape[1]
    hit = iota((n, n_groups), 1) == row // 2
    limit = jnp.sum(
        jnp.where(hit, count_ref[...].astype(F32), 0.0), axis=1, keepdims=True
    )
    return (row % 2).astype(F32) < limit


def half_sums(n_zh, n_zl, side, wide, count_ref, flat_ref, out_ref):
    _, depth, features = flat_ref.shape
    total = wide[0].shape[1]
    half = total // 2
    i = iota((half, 1), 0)
    d = i // (2 * n_zh)
    far = i % (2 * n_zh) // 2
    low = at_place(low_order(n_zl), d % n_zl)
    high = at_place(high_order(n_zh), far)
    row = ((high * n_zl + low) * 2 + d // n_zl) * 4 + side * 2 + i % 2
    is_text = text_column(row, count_ref)
    is_mine = (iota((half, depth), 1) % 2 == 0) == is_text
    pick = (iota((half, total), 1) == row).astype(BF16)

    def product(w, at):
        left = jnp.where(is_mine, dot(pick, wide[w], ((1,), (1,))), 0.0).astype(BF16)
        return dot(left, flat_ref[at])

    out_ref[:, :features] = product(0, 2).astype(out_ref.dtype)
    out_ref[:, features:] = (product(1, 0) + product(2, 1)).astype(out_ref.dtype)


def send_sums_kernel(n_zh, n_zl, core_ref, rows_ref, count_ref, flat_ref, out_ref, wide_ref):
    width = flat_ref.shape[1] // 2
    wide = unpacked(width, rows_ref)
    half_sums(n_zh, n_zl, 1 - core_ref[0], wide, count_ref, flat_ref, out_ref)
    for w in range(3):
        wide_ref[w] = wide[w]


def keep_sums_kernel(n_zh, n_zl, core_ref, wide_ref, count_ref, flat_ref, out_ref):
    wide = [wide_ref[w] for w in range(3)]
    half_sums(n_zh, n_zl, core_ref[0], wide, count_ref, flat_ref, out_ref)


def add_kernel(keep_ref, got_ref, out_ref):
    out_ref[...] = (keep_ref[...] + got_ref[...].astype(F32)).astype(BF16)


def weight_grads_kernel(wide_ref, count_ref, tok_ref, cot_ref, gate_ref, up_ref, down_ref):
    total, features = tok_ref.shape
    width = gate_ref.shape[0]
    is_text = text_lanes(count_ref, total)
    is_mine = (iota((2 * width, total), 0) % 2 == 0) == is_text
    for w, (left, out) in enumerate(((cot_ref, down_ref), (tok_ref, gate_ref), (tok_ref, up_ref))):
        rows = jnp.where(is_mine, wide_ref[w].astype(F32), 0.0).astype(BF16)
        out[...] = dot(rows, left[...]).reshape(width, 2, features)


def program(n_zh, n_zl, n_tensor):
    near, far = groups_of(n_zh, n_zl)
    n_near = 2 * n_zl

    def on_device(tokens, cotangent, text_count, w_gate, w_up, w_down):
        total, features = tokens.shape
        width = w_gate.shape[2]
        half = total // 2
        lanes = min(total, LANES)
        counts = text_count.reshape(1, -1)
        gate_w = jnp.transpose(w_gate, (2, 0, 1))
        up_w = jnp.transpose(w_up, (2, 0, 1))
        down_w = jnp.transpose(w_down, (1, 0, 2))
        core = (lax.axis_index("dp") % 2).astype(I32).reshape(1)
        params = pltpu.CompilerParams(vmem_limit_bytes=24 * 1024 * 1024)
        n_dp = 4 * n_zh * n_zl
        pairs = [(i, i ^ 1) for i in range(n_dp)]
        in_hbm = [
            pltpu.with_memory_space_constraint(x, pltpu.HBM)
            for x in (tokens, cotangent, counts, gate_w, up_w, down_w)
        ]
        chunks = total // lanes
        depth = packed_rows(width, n_tensor, chunks)
        partial, flat = pl.pallas_call(
            partial_kernel,
            out_shape=(
                jax.ShapeDtypeStruct((n_tensor, depth, lanes), F32),
                jax.ShapeDtypeStruct((3, 2 * width, features), BF16),
            ),
            in_specs=[SMEM] + [HBM] * 6,
            out_specs=(VMEM, VMEM),
            scratch_shapes=[
                pltpu.VMEM((total, features), BF16),
                pltpu.VMEM((total, features), BF16),
                pltpu.VMEM(counts.shape, I32),
                pltpu.VMEM((width, 2, features), BF16),
                pltpu.VMEM((width, 2, features), BF16),
                pltpu.VMEM((width, 2, features), BF16),
                pltpu.VMEM((chunks, 2 * n_tensor * per_share(width, n_tensor), lanes), F32),
                pltpu.SemaphoreType.DMA((6,)),
            ],
            compiler_params=params,
            name="partial_sums",
        )(core, *in_hbm)
        shares = lax.all_to_all(partial, "tensor", 0, 0)
        copies = pl.pallas_call(
            functools.partial(rows_kernel, width),
            out_shape=jax.ShapeDtypeStruct(shares.shape, BF16),
            in_specs=[VMEM],
            out_specs=VMEM,
            compiler_params=params,
            name="hidden_rows",
        )(shares)
        rows = lax.all_to_all(copies, "tensor", 0, 0)

        cost = pl.CostEstimate(
            flops=12 * half * width * features, bytes_accessed=4 << 20, transcendentals=0
        )
        send, wide = pl.pallas_call(
            functools.partial(send_sums_kernel, n_zh, n_zl),
            out_shape=(
                jax.ShapeDtypeStruct((half, 2 * features), BF16),
                jax.ShapeDtypeStruct((3, 2 * width, total), BF16),
            ),
            in_specs=[SMEM] + [VMEM] * 3,
            out_specs=(VMEM, VMEM),
            compiler_params=params,
            cost_estimate=cost,
            name="other_core_sums",
        )(core, rows, counts, flat)
        keep = pl.pallas_call(
            functools.partial(keep_sums_kernel, n_zh, n_zl),
            out_shape=jax.ShapeDtypeStruct((half, 2 * features), F32),
            in_specs=[SMEM] + [VMEM] * 3,
            out_specs=VMEM,
            compiler_params=params,
            cost_estimate=cost,
            name="own_core_sums",
        )(core, wide, counts, flat)
        got = lax.ppermute(send, "dp", pairs)
        chip = pl.pallas_call(
            add_kernel,
            out_shape=jax.ShapeDtypeStruct((half, 2 * features), BF16),
            in_specs=[VMEM] * 2,
            out_specs=VMEM,
            compiler_params=params,
            name="chip_sums",
        )(keep, got)
        chip = chip.reshape(n_near, half // n_near, 2 * features)
        parts = lax.all_to_all(chip, "dp", 0, 0, axis_index_groups=near)
        grads = pl.pallas_call(
            weight_grads_kernel,
            out_shape=(jax.ShapeDtypeStruct((width, 2, features), F32),) * 3,
            in_specs=[VMEM] * 4,
            out_specs=(VMEM,) * 3,
            compiler_params=params,
            cost_estimate=pl.CostEstimate(
                flops=12 * total * width * features, bytes_accessed=4 << 20, transcendentals=0
            ),
            name="weight_grads",
        )(wide, counts, tokens, cotangent)
        mine = jnp.sum(parts.astype(F32), axis=0).astype(BF16)
        mine = mine.reshape(n_zh, 2, 2 * features)
        mine, gate_g, up_g, down_g = lax.optimization_barrier((mine,) + tuple(grads))
        parts = lax.all_to_all(mine, "dp", 0, 0, axis_index_groups=far)
        out = jnp.sum(parts.astype(F32), axis=0).astype(BF16)
        return (
            out[:, :features],
            out[:, features:],
            jnp.transpose(gate_g, (1, 2, 0)),
            jnp.transpose(up_g, (1, 2, 0)),
            jnp.transpose(down_g, (1, 0, 2)),
        )

    return on_device


def solution(mesh):
    n_zh, n_zl = dp_parts(mesh.shape["dp"])
    return jax.shard_map(
        program(n_zh, n_zl, mesh.shape["tensor"]),
        mesh=mesh,
        in_specs=(
            P(None, "tensor"),
            P(None, "tensor"),
            P(),
            P(None, "tensor", "dp"),
            P(None, "tensor", "dp"),
            P(None, "dp", "tensor"),
        ),
        out_specs=(
            P("dp", "tensor"),
            P("dp", "tensor"),
            P(None, "tensor", "dp"),
            P(None, "tensor", "dp"),
            P(None, "dp", "tensor"),
        ),
        check_vma=False,
    )
```

```python
import functools

import jax
import jax.numpy as jnp
from jax import lax
from jax.experimental import pallas as pl
from jax.experimental.pallas import tpu as pltpu
from jax.sharding import PartitionSpec as P

BF16 = jnp.bfloat16
F32 = jnp.float32
I32 = jnp.int32
LANES = 128
VMEM = pl.BlockSpec(memory_space=pltpu.VMEM)
SMEM = pl.BlockSpec(memory_space=pltpu.SMEM)
HBM = pl.BlockSpec(memory_space=pltpu.HBM)


def dp_parts(n):
    z = n // 4
    z_lo = 4 if z >= 16 else 2
    return z // z_lo, z_lo


def low_order(n_zl, core):
    order = sorted(range(n_zl), key=lambda low: (abs(low - n_zl // 2), low))
    return [n_zl - 1 - low for low in order] if core else order


def high_order(n_zh):
    return sorted(range(n_zh), key=lambda h: (h != n_zh // 2, min(h, n_zh - h), h))


def at_place(order, place):
    value = jnp.zeros_like(place)
    for k, entry in enumerate(order):
        value = jnp.where(place == k, entry, value)
    return value


def groups_of(n_zh, n_zl):
    near = [
        [((h * n_zl + low) * 2 + x) * 2 + c for x in (c, 1 - c) for low in low_order(n_zl, c)]
        for h in range(n_zh)
        for c in range(2)
    ]
    far = [
        [((h * n_zl + low) * 2 + x) * 2 + c for h in high_order(n_zh)]
        for low in range(n_zl)
        for x in range(2)
        for c in range(2)
    ]
    return near, far


def iota(shape, dim):
    return lax.broadcasted_iota(I32, shape, dim)


def dot(left, right, dims=((1,), (0,))):
    return lax.dot_general(left, right, (dims, ((), ())), preferred_element_type=F32)


def per_share(width, n):
    return -(-width // n)


def packed_rows(width, n, chunks):
    return -(-3 * chunks * per_share(width, n) // 8) * 8


def partial_kernel(core_ref, tok_hbm, cot_hbm, count_hbm, gate_hbm, up_hbm, down_hbm, out_ref, flat_ref, tok, cot, count_ref, gate, up, down, both, sems):
    pairs = (
        (count_hbm, count_ref),
        (tok_hbm, tok),
        (gate_hbm, gate),
        (up_hbm, up),
        (cot_hbm, cot),
        (down_hbm, down),
    )
    copies = [pltpu.make_async_copy(src, dst, sems.at[k]) for k, (src, dst) in enumerate(pairs)]
    for copy in copies:
        copy.start()
    total, features = tok.shape
    width = gate.shape[0]
    shares = out_ref.shape[0]
    part = per_share(width, shares)
    chunks, depth, lanes = both.shape
    out_ref[...] = jnp.zeros_like(out_ref)
    both[...] = jnp.zeros_like(both)
    copies[0].wait()
    is_text = text_lanes(count_ref, total)
    for w, (left, weight, needs) in enumerate(
        ((tok, gate, (1, 2)), (tok, up, (3,)), (cot, down, (4, 5)))
    ):
        for k in needs:
            copies[k].wait()
        rows = weight[...].reshape(2 * width, features)
        flat_ref[w] = rows
        products = dot(rows, left[...], ((1,), (1,)))
        for c in range(chunks):
            here = slice(c * lanes, (c + 1) * lanes)
            both[c, 0 : 2 * width, :] = products[:, here]
            at = (3 * c + w) * part
            for share in range(shares):
                text = both[c, pl.ds(2 * share, part, 2 * shares), :]
                image = both[c, pl.ds(2 * share + 1, part, 2 * shares), :]
                out_ref[share, at : at + part, :] = jnp.where(is_text[:, here], text, image)


def rows_kernel(width, share_ref, out_ref):
    shares, depth, _ = share_ref.shape
    part = per_share(width, shares)
    chunks = depth // (3 * part)
    total = share_ref[0]
    for k in range(1, shares):
        total = total + share_ref[k]
    pieces = []
    for c in range(chunks):
        at = 3 * c * part
        gate = total[at : at + part]
        up = total[at + part : at + 2 * part]
        grad_hidden = total[at + 2 * part : at + 3 * part]
        sig = jax.nn.sigmoid(gate)
        act = gate * sig
        pieces += [
            act * up,
            grad_hidden * up * sig * (1.0 + gate * (1.0 - sig)),
            grad_hidden * act,
        ]
    pad = depth - 3 * chunks * part
    if pad:
        pieces.append(jnp.zeros((pad, total.shape[1]), F32))
    rows = jnp.concatenate(pieces, axis=0).astype(BF16)
    for k in range(shares):
        out_ref[k] = rows


def unpacked(width, rows_ref):
    shares, depth, lanes = rows_ref.shape
    part = per_share(width, shares)
    room = -(-part // 16) * 16
    chunks = depth // (3 * part)
    unit = iota((2 * width, shares * room), 0) // 2
    column = iota((2 * width, shares * room), 1)
    move = (column == unit % shares * room + unit // shares).astype(BF16)
    rows = rows_ref[...].astype(F32)
    pad = jnp.zeros((shares, room - part, lanes), F32)

    def piece(c, w):
        at = (3 * c + w) * part
        some = jnp.concatenate((rows[:, at : at + part], pad), axis=1)
        return dot(move, some.reshape(shares * room, lanes).astype(BF16)).astype(BF16)

    return [jnp.concatenate([piece(c, w) for c in range(chunks)], axis=1) for w in range(3)]


def text_lanes(count_ref, total):
    n_groups = count_ref.shape[1]
    spread = (iota((n_groups, total), 1) // 2 == iota((n_groups, total), 0)).astype(BF16)
    counts = jnp.broadcast_to(count_ref[...].astype(F32), (8, n_groups)).astype(BF16)
    limit = dot(counts, spread)[0:1, :]
    return (iota((1, total), 1) % 2).astype(F32) < limit


def text_column(row, count_ref):
    n, n_groups = row.shape[0], count_ref.shape[1]
    hit = iota((n, n_groups), 1) == row // 2
    limit = jnp.sum(
        jnp.where(hit, count_ref[...].astype(F32), 0.0), axis=1, keepdims=True
    )
    return (row % 2).astype(F32) < limit


def half_sums(n_zh, n_zl, side, wide, count_ref, flat_ref, out_ref):
    _, depth, features = flat_ref.shape
    total = wide[0].shape[1]
    half = total // 2
    i = iota((half, 1), 0)
    d = i // (2 * n_zh)
    far = i % (2 * n_zh) // 2
    low = jnp.where(
        side == 0,
        at_place(low_order(n_zl, 0), d % n_zl),
        at_place(low_order(n_zl, 1), d % n_zl),
    )
    x_high = jnp.where(side == 0, d // n_zl, 1 - d // n_zl)
    high = at_place(high_order(n_zh), far)
    row = ((high * n_zl + low) * 2 + x_high) * 4 + side * 2 + i % 2
    is_text = text_column(row, count_ref)
    is_mine = (iota((half, depth), 1) % 2 == 0) == is_text
    pick = (iota((half, total), 1) == row).astype(BF16)

    def product(w, at):
        left = jnp.where(is_mine, dot(pick, wide[w], ((1,), (1,))), 0.0).astype(BF16)
        return dot(left, flat_ref[at])

    out_ref[:, :features] = product(0, 2).astype(out_ref.dtype)
    out_ref[:, features:] = (product(1, 0) + product(2, 1)).astype(out_ref.dtype)


def send_sums_kernel(n_zh, n_zl, core_ref, rows_ref, count_ref, flat_ref, out_ref, wide_ref):
    width = flat_ref.shape[1] // 2
    wide = unpacked(width, rows_ref)
    half_sums(n_zh, n_zl, 1 - core_ref[0], wide, count_ref, flat_ref, out_ref)
    for w in range(3):
        wide_ref[w] = wide[w]


def keep_sums_kernel(n_zh, n_zl, core_ref, wide_ref, count_ref, flat_ref, out_ref):
    wide = [wide_ref[w] for w in range(3)]
    half_sums(n_zh, n_zl, core_ref[0], wide, count_ref, flat_ref, out_ref)


def add_kernel(keep_ref, got_ref, out_ref):
    out_ref[...] = (keep_ref[...] + got_ref[...].astype(F32)).astype(BF16)


def weight_grads_kernel(wide_ref, count_ref, tok_ref, cot_ref, gate_ref, up_ref, down_ref):
    total, features = tok_ref.shape
    width = gate_ref.shape[0]
    is_text = text_lanes(count_ref, total)
    is_mine = (iota((2 * width, total), 0) % 2 == 0) == is_text
    for w, (left, out) in enumerate(((cot_ref, down_ref), (tok_ref, gate_ref), (tok_ref, up_ref))):
        rows = jnp.where(is_mine, wide_ref[w].astype(F32), 0.0).astype(BF16)
        out[...] = dot(rows, left[...]).reshape(width, 2, features)


def program(n_zh, n_zl, n_tensor):
    near, far = groups_of(n_zh, n_zl)
    n_near = 2 * n_zl

    def on_device(tokens, cotangent, text_count, w_gate, w_up, w_down):
        total, features = tokens.shape
        width = w_gate.shape[2]
        half = total // 2
        lanes = min(total, LANES)
        counts = text_count.reshape(1, -1)
        gate_w = jnp.transpose(w_gate, (2, 0, 1))
        up_w = jnp.transpose(w_up, (2, 0, 1))
        down_w = jnp.transpose(w_down, (1, 0, 2))
        core = (lax.axis_index("dp") % 2).astype(I32).reshape(1)
        params = pltpu.CompilerParams(vmem_limit_bytes=24 * 1024 * 1024)
        n_dp = 4 * n_zh * n_zl
        pairs = [(i, i ^ 1) for i in range(n_dp)]
        in_hbm = [
            pltpu.with_memory_space_constraint(x, pltpu.HBM)
            for x in (tokens, cotangent, counts, gate_w, up_w, down_w)
        ]
        chunks = total // lanes
        depth = packed_rows(width, n_tensor, chunks)
        partial, flat = pl.pallas_call(
            partial_kernel,
            out_shape=(
                jax.ShapeDtypeStruct((n_tensor, depth, lanes), F32),
                jax.ShapeDtypeStruct((3, 2 * width, features), BF16),
            ),
            in_specs=[SMEM] + [HBM] * 6,
            out_specs=(VMEM, VMEM),
            scratch_shapes=[
                pltpu.VMEM((total, features), BF16),
                pltpu.VMEM((total, features), BF16),
                pltpu.VMEM(counts.shape, I32),
                pltpu.VMEM((width, 2, features), BF16),
                pltpu.VMEM((width, 2, features), BF16),
                pltpu.VMEM((width, 2, features), BF16),
                pltpu.VMEM((chunks, 2 * n_tensor * per_share(width, n_tensor), lanes), F32),
                pltpu.SemaphoreType.DMA((6,)),
            ],
            compiler_params=params,
            name="partial_sums",
        )(core, *in_hbm)
        shares = lax.all_to_all(partial, "tensor", 0, 0)
        copies = pl.pallas_call(
            functools.partial(rows_kernel, width),
            out_shape=jax.ShapeDtypeStruct(shares.shape, BF16),
            in_specs=[VMEM],
            out_specs=VMEM,
            compiler_params=params,
            name="hidden_rows",
        )(shares)
        rows = lax.all_to_all(copies, "tensor", 0, 0)

        cost = pl.CostEstimate(
            flops=12 * half * width * features, bytes_accessed=4 << 20, transcendentals=0
        )
        send, wide = pl.pallas_call(
            functools.partial(send_sums_kernel, n_zh, n_zl),
            out_shape=(
                jax.ShapeDtypeStruct((half, 2 * features), BF16),
                jax.ShapeDtypeStruct((3, 2 * width, total), BF16),
            ),
            in_specs=[SMEM] + [VMEM] * 3,
            out_specs=(VMEM, VMEM),
            compiler_params=params,
            cost_estimate=cost,
            name="other_core_sums",
        )(core, rows, counts, flat)
        keep = pl.pallas_call(
            functools.partial(keep_sums_kernel, n_zh, n_zl),
            out_shape=jax.ShapeDtypeStruct((half, 2 * features), F32),
            in_specs=[SMEM] + [VMEM] * 3,
            out_specs=VMEM,
            compiler_params=params,
            cost_estimate=cost,
            name="own_core_sums",
        )(core, wide, counts, flat)
        got = lax.ppermute(send, "dp", pairs)
        chip = pl.pallas_call(
            add_kernel,
            out_shape=jax.ShapeDtypeStruct((half, 2 * features), BF16),
            in_specs=[VMEM] * 2,
            out_specs=VMEM,
            compiler_params=params,
            name="chip_sums",
        )(keep, got)
        chip = chip.reshape(n_near, half // n_near, 2 * features)
        parts = lax.all_to_all(chip, "dp", 0, 0, axis_index_groups=near)
        grads = pl.pallas_call(
            weight_grads_kernel,
            out_shape=(jax.ShapeDtypeStruct((width, 2, features), F32),) * 3,
            in_specs=[VMEM] * 4,
            out_specs=(VMEM,) * 3,
            compiler_params=params,
            cost_estimate=pl.CostEstimate(
                flops=12 * total * width * features, bytes_accessed=4 << 20, transcendentals=0
            ),
            name="weight_grads",
        )(wide, counts, tokens, cotangent)
        mine = jnp.sum(parts.astype(F32), axis=0).astype(BF16)
        mine = mine.reshape(n_zh, 2, 2 * features)
        mine, gate_g, up_g, down_g = lax.optimization_barrier((mine,) + tuple(grads))
        parts = lax.all_to_all(mine, "dp", 0, 0, axis_index_groups=far)
        out = jnp.sum(parts.astype(F32), axis=0).astype(BF16)
        return (
            out[:, :features],
            out[:, features:],
            jnp.transpose(gate_g, (1, 2, 0)),
            jnp.transpose(up_g, (1, 2, 0)),
            jnp.transpose(down_g, (1, 0, 2)),
        )

    return on_device


def solution(mesh):
    n_zh, n_zl = dp_parts(mesh.shape["dp"])
    return jax.shard_map(
        program(n_zh, n_zl, mesh.shape["tensor"]),
        mesh=mesh,
        in_specs=(
            P(None, "tensor"),
            P(None, "tensor"),
            P(),
            P(None, "tensor", "dp"),
            P(None, "tensor", "dp"),
            P(None, "dp", "tensor"),
        ),
        out_specs=(
            P("dp", "tensor"),
            P("dp", "tensor"),
            P(None, "tensor", "dp"),
            P(None, "tensor", "dp"),
            P(None, "dp", "tensor"),
        ),
        check_vma=False,
    )
```
